32 devices in a mesh: dp: 8 (over z, core), tensor: 4 (over y, x).
Axes of the slice: x: 2, y: 2, z: 4, core: 2. Of those that a mesh axis runs over, the one named last changes fastest.
Arguments:
- attention_inputs: bfloat16 [5120, 8192], P('dp', 'tensor'), may hold values from -6 to 6
- mixing_inputs: bfloat16 [5120, 8192], P('dp', 'tensor'), may hold values from -6 to 6
- feedforward_inputs: bfloat16 [5120, 8192], P('dp', 'tensor'), may hold values from -6 to 6
- hidden_inputs: bfloat16 [5120, 28672], P('dp', 'tensor'), may hold values from -6 to 6
- query_grads: bfloat16 [5120, 8192], P('dp', 'tensor'), may hold values from -6 to 6
- keyvalue_grads: bfloat16 [2, 5120, 1024], P(None, 'dp', 'tensor'), may hold values from -6 to 6
- mixing_grads: bfloat16 [5120, 8192], P('dp', 'tensor'), may hold values from -6 to 6
- gateup_grads: bfloat16 [2, 5120, 28672], P(None, 'dp', 'tensor'), may hold values from -6 to 6
- down_grads: bfloat16 [5120, 8192], P('dp', 'tensor'), may hold values from -6 to 6
- input_bases: bfloat16 [3, 64, 8192], P(None, None, 'tensor'), may hold values from -0.0625 to 0.0625
- hidden_basis: bfloat16 [64, 28672], P(None, 'tensor'), may hold values from -0.03125 to 0.03125
- output_bases: bfloat16 [3, 64, 8192], P(None, None, 'tensor'), may hold values from -0.0625 to 0.0625
- keyvalue_bases: bfloat16 [2, 64, 1024], P(None, None, 'tensor'), may hold values from -0.1875 to 0.1875
- gateup_bases: bfloat16 [2, 64, 28672], P(None, None, 'tensor'), may hold values from -0.03125 to 0.03125
- eigenvalues: float32 [7, 64, 64], replicated, may hold values from 0.05 to 5
- example_lengths: int32 [8, 8], P('dp'), may hold values from 1 to 320, 640 in all within a row
- test_gradients: bfloat16 [1024, 28672], P(('dp', 'tensor')), may hold values from -0.0029907227 to 0.0029907227
Outputs:
- scores: float32 [1024, 64], P(('dp', 'tensor'))
The draws below stay inside these ranges and needn't reach their ends.
Inputs may be any that keep to these rules, and one draw needn't show every extreme that they name: `example_lengths`: each row holds the lengths of the 8 examples that fill the 640 tokens of one index of dp, in order; they sum to 640, and the longest in every row is exactly 320.
All inputs are finite; a program needn't handle non-finite values.
Results may differ from the reference program's by a relative error of at most 0.0029.
Values may be sent and summed in bfloat16 or wider, within the bound.
A program may use at most 128 MiB of HBM per device.

```python
import math
import jax
import jax.numpy as jnp
import numpy as np
from jax import lax

D = 8192
FF = 28672
KV = 1024
R = 64
EX_DEV = 8
TOK_DEV = 640
EX_LEN = 320
GROUPS = 8
TOKENS = 5120
QUERIES = 1024
FLAT = 28672


def levels(rng, extent, pieces, smallest, top_value):
    level, own = 1.0, jax.random.fold_in(rng, 6)
    for dim, parts in pieces:
        draws = jnp.exp(jax.random.uniform(jax.random.fold_in(own, dim), (parts,), jnp.float32, smallest / len(pieces), top_value / len(pieces)))
        level = level * jnp.repeat(draws, extent[dim] // parts).reshape([-1 if axis == dim else 1 for axis in range(len(extent))])
    return level


def split_up(amount, total, bound, lean):
    loads = [(1 << 20) // math.isqrt(standing ** lean) + 1 for standing in range(2, amount + 1)]
    surplus, counts = total - bound - (amount - 1), [1] * (amount - 1)
    while surplus > 0:
        candidates = [i for i in range(amount - 1) if counts[i] < bound]
        pool, budget = sum([loads[i] for i in candidates]), surplus
        for i in candidates:
            addition = min(bound - counts[i], max(1, budget * loads[i] // pool), surplus)
            counts[i] = counts[i] + addition
            surplus = surplus - addition
    return np.array([bound] + counts)


def uneven_parts(stream_key, count, total, bound, slope):
    if count == 2:
        one = jax.random.randint(stream_key, (), max(1, total - bound), min(bound, total - 1) + 1)
        return jnp.stack([one, total - one])
    lengths = jnp.asarray(split_up(count, total, bound, slope), jnp.int32)
    pairs = (count - 1) // 2
    giver, receiver = lengths[1:1 + 2 * pairs:2], lengths[2:2 + 2 * pairs:2]
    margin = jnp.minimum(giver - 1, bound - receiver)
    shifted = jax.random.randint(jax.random.fold_in(stream_key, 1), (pairs,), 0, 1 << 20) % (margin + 1)
    lengths = lengths.at[1:1 + 2 * pairs:2].set(giver - shifted).at[2:2 + 2 * pairs:2].set(receiver + shifted)
    return lengths[jax.random.permutation(jax.random.fold_in(stream_key, 2), count)]


def scatter_about(rng, extent, scale, bound, cuts=(), kind=jnp.bfloat16):
    gain = levels(rng, extent, cuts, -0.22, 0.18) if cuts else 1.0
    result = jax.random.normal(rng, extent, jnp.float32) * scale * gain
    return jnp.minimum(jnp.maximum(result, -bound), bound).astype(kind)


def setup_inputs(seed: int = 0) -> dict:
    streams_of = jax.random.split(jax.random.key(seed), 18)
    attention_inputs = scatter_about(streams_of[0], (TOKENS, D), 1.0, 6.0, ((0, 8), (1, 4)))
    mixing_inputs = scatter_about(streams_of[1], (TOKENS, D), 1.0, 6.0, ((0, 8), (1, 4)))
    feedforward_inputs = scatter_about(streams_of[2], (TOKENS, D), 1.0, 6.0, ((0, 8), (1, 4)))
    hidden_inputs = scatter_about(streams_of[3], (TOKENS, FF), 1.0, 6.0, ((0, 8), (1, 4)))
    query_grads = scatter_about(streams_of[4], (TOKENS, D), 1.0, 6.0, ((0, 8), (1, 4)))
    keyvalue_grads = scatter_about(streams_of[5], (2, TOKENS, KV), 1.0, 6.0, ((1, 8), (2, 4)))
    mixing_grads = scatter_about(streams_of[6], (TOKENS, D), 1.0, 6.0, ((0, 8), (1, 4)))
    gateup_grads = scatter_about(streams_of[7], (2, TOKENS, FF), 1.0, 6.0, ((1, 8), (2, 4)))
    down_grads = scatter_about(streams_of[8], (TOKENS, D), 1.0, 6.0, ((0, 8), (1, 4)))
    input_bases = scatter_about(streams_of[9], (3, R, D), D ** -0.5, 0.0625, ((2, 4),))
    hidden_basis = scatter_about(streams_of[10], (R, FF), FF ** -0.5, 0.03125, ((1, 4),))
    output_bases = scatter_about(streams_of[11], (3, R, D), D ** -0.5, 0.0625, ((2, 4),))
    keyvalue_bases = scatter_about(streams_of[12], (2, R, KV), KV ** -0.5, 0.1875, ((2, 4),))
    gateup_bases = scatter_about(streams_of[13], (2, R, FF), FF ** -0.5, 0.03125, ((2, 4),))
    eigenvalues = jnp.clip(jnp.exp(jax.random.uniform(streams_of[14], (7, R, R), jnp.float32, math.log(0.05), math.log(5.0))), 0.05, 5.0)
    example_lengths = jax.vmap(lambda own: uneven_parts(own, EX_DEV, TOK_DEV, EX_LEN, 1))(jax.random.split(streams_of[15], GROUPS)).reshape((GROUPS, EX_DEV)).astype(jnp.int32)
    test_gradients = scatter_about(streams_of[16], (QUERIES, FLAT), 0.0005, 0.0029907227, ((0, 32),))
    return dict(attention_inputs=attention_inputs, mixing_inputs=mixing_inputs, feedforward_inputs=feedforward_inputs, hidden_inputs=hidden_inputs, query_grads=query_grads, keyvalue_grads=keyvalue_grads, mixing_grads=mixing_grads, gateup_grads=gateup_grads, down_grads=down_grads, input_bases=input_bases, hidden_basis=hidden_basis, output_bases=output_bases, keyvalue_bases=keyvalue_bases, gateup_bases=gateup_bases, eigenvalues=eigenvalues, example_lengths=example_lengths, test_gradients=test_gradients)


damping = 0.1


def project_rows(basis_rows, features):
    return lax.dot_general(basis_rows, features, (((1,), (1,)), ((), ())), preferred_element_type=jnp.float32)


def all_projections(attention_inputs, mixing_inputs, feedforward_inputs, hidden_inputs, query_grads, keyvalue_grads, mixing_grads, gateup_grads, down_grads, input_bases, hidden_basis, output_bases, keyvalue_bases, gateup_bases):
    inputs_side = [project_rows(input_bases[0], attention_inputs), project_rows(input_bases[1], mixing_inputs), project_rows(input_bases[2], feedforward_inputs), project_rows(hidden_basis, hidden_inputs)]
    outputs_side = [project_rows(output_bases[0], query_grads), project_rows(keyvalue_bases[0], keyvalue_grads[0]), project_rows(keyvalue_bases[1], keyvalue_grads[1]), project_rows(output_bases[1], mixing_grads), project_rows(gateup_bases[0], gateup_grads[0]), project_rows(gateup_bases[1], gateup_grads[1]), project_rows(output_bases[2], down_grads)]
    return jnp.stack(inputs_side + outputs_side)


def example_gradients(inputs, outputs, lengths_row):
    columns = inputs.shape[2]
    finish = jnp.cumsum(lengths_row).astype(jnp.int32)
    begins = (finish - lengths_row).astype(jnp.int32)
    position = jnp.arange(columns, dtype=jnp.int32)
    member = jnp.logical_and(position[None, :] >= begins[:, None], position[None, :] < finish[:, None]).astype(inputs.dtype)
    masked = member[:, None, None, :] * inputs[None]
    sources = (0, 0, 0, 1, 2, 2, 3)
    blocks = []
    for module in range(7):
        blocks.append(jnp.einsum("ot,eit->eoi", outputs[module], masked[:, sources[module]], precision=lax.Precision.HIGHEST))
    return jnp.stack(blocks, axis=1)


def reference(attention_inputs, mixing_inputs, feedforward_inputs, hidden_inputs, query_grads, keyvalue_grads, mixing_grads, gateup_grads, down_grads, input_bases, hidden_basis, output_bases, keyvalue_bases, gateup_bases, eigenvalues, example_lengths, test_gradients):
    projected = all_projections(attention_inputs, mixing_inputs, feedforward_inputs, hidden_inputs, query_grads, keyvalue_grads, mixing_grads, gateup_grads, down_grads, input_bases, hidden_basis, output_bases, keyvalue_bases, gateup_bases)
    group_count = example_lengths.shape[0]
    per_group = projected.reshape(11, R, group_count, TOK_DEV).transpose(2, 0, 1, 3)
    gradients = lax.map(lambda pair: example_gradients(pair[0][:4], pair[0][4:], pair[1]), (per_group, example_lengths))
    gradients = gradients.reshape(-1, 7, R, R)
    scaled = gradients / (eigenvalues[None] + damping)
    flattened = scaled.astype(jnp.bfloat16).reshape(gradients.shape[0], -1)
    return lax.dot_general(test_gradients, flattened, (((1,), (1,)), ((), ())), preferred_element_type=jnp.float32)
```

```python
import functools

import jax
import jax.numpy as jnp
from jax import lax
from jax.experimental import pallas as pl
from jax.experimental.pallas import tpu as pltpu
from jax.sharding import PartitionSpec as P

damping = 0.1
MESH = pl.DeviceIdType.MESH
GROUP = 4
CHUNK = 128
SLOTS = 4

SOURCES = (0, 0, 0, 1, 2, 2, 3)
NT = (((1,), (1,)), ((), ()))


def input_pair(index, shares, modules, rank):
    start = index * (modules * rank // shares)
    return min(SOURCES[start // rank], max(SOURCES) - 1)


def body(
    dp, shares, attention, mixing, feedforward, hidden, query, keyvalue, mixing_g, gateup, down,
    input_bases, hidden_basis, output_bases, keyvalue_bases, gateup_bases, eigen, lengths, test,
    scores,
    narrow, wide, kv, bases_in, basis_hidden, bases_out, bases_kv, bases_gu,
    part_in, part_out, got_in, got_out, tests, r_hi, r_lo, grads, scaled_f, scaled, gathered, spread, partial, got_partial,
    load_sem, base_sem, in_send, in_recv, out_send, out_recv, test_send, test_recv, test_local,
    grad_send, grad_recv, grad_local, fin_send, fin_recv,
):
    me_dp, me = lax.axis_index("dp"), lax.axis_index("tensor")
    total = dp * shares
    ident = me_dp * shares + me
    tokens = attention.shape[0]
    rank = input_bases.shape[1]
    modules = len(SOURCES)
    rows = modules * rank // shares
    examples = lengths.shape[1]
    lane = me_dp % GROUP
    group_at = me_dp - lane
    width = tests.shape[2] // shares
    pairs = rows // 2
    piece = pairs // GROUP

    units = [
        ("n", attention, None, bases_in, 0, 0),
        ("n", mixing, None, bases_in, 1, 1),
        ("n", feedforward, None, bases_in, 2, 2),
        ("n", query, None, bases_out, 0, 4),
        ("k", keyvalue, None, bases_kv, None, 5),
        ("n", mixing_g, None, bases_out, 1, 7),
        ("n", down, None, bases_out, 2, 10),
        ("w", hidden, None, basis_hidden, None, 3),
        ("w", gateup, 0, bases_gu, 0, 8),
        ("w", gateup, 1, bases_gu, 1, 9),
    ]
    steps = []
    count = {"n": 0, "w": 0, "k": 0}
    for kind, array, at, basis, basis_at, unit in units:
        for chunk in range(tokens // CHUNK if kind == "w" else 1):
            slot = count[kind] % SLOTS
            count[kind] += 1
            steps.append((kind, array, at, basis, basis_at, unit, chunk, slot))
    last_chunk = tokens // CHUNK - 1

    def load(number):
        kind, array, at, _, _, _, chunk, slot = steps[number]
        if kind == "n":
            return pltpu.make_async_copy(array, narrow.at[slot], load_sem.at[number % SLOTS])
        if kind == "k":
            return pltpu.make_async_copy(array, kv, load_sem.at[number % SLOTS])
        source = array if at is None else array.at[at]
        return pltpu.make_async_copy(
            source.at[pl.ds(chunk * CHUNK, CHUNK)], wide.at[slot], load_sem.at[number % SLOTS]
        )

    base_copies = [
        pltpu.make_async_copy(a, b, base_sem.at[i])
        for i, (a, b) in enumerate(
            [
                (input_bases, bases_in),
                (output_bases, bases_out),
                (keyvalue_bases, bases_kv),
                (hidden_basis, basis_hidden),
                (gateup_bases, bases_gu),
            ]
        )
    ]
    based = {}

    def need_basis(basis):
        for i, ref in enumerate([bases_in, bases_out, bases_kv, basis_hidden, bases_gu]):
            if ref is basis and i not in based:
                base_copies[i].wait()
                based[i] = True

    base_copies[0].start()
    for number in range(SLOTS):
        load(number).start()
    for copy in base_copies[1:]:
        copy.start()

    barrier = pltpu.get_barrier_semaphore()

    def greet(k, carry):
        other = (ident + k) % total
        pl.semaphore_signal(
            barrier, inc=1, device_id=(other // shares, other % shares), device_id_type=MESH
        )
        return carry

    lax.fori_loop(1, total, greet, 0)

    def test_copy(j, t, source_lane):
        return pltpu.make_async_remote_copy(
            src_ref=test.at[:, pl.ds(pl.multiple_of((t * GROUP + j) * width, 128), width)],
            dst_ref=tests.at[source_lane, :, pl.ds(t * width, width)],
            send_sem=test_send.at[j, t],
            recv_sem=test_recv.at[source_lane, t],
            device_id=(group_at + j, me),
            device_id_type=MESH,
        )

    def own_test(t):
        return pltpu.make_async_copy(
            test.at[:, pl.ds(pl.multiple_of((t * GROUP + lane) * width, 128), width)],
            tests.at[lane, :, pl.ds(t * width, width)],
            test_local.at[t],
        )

    def in_copy(unit, target, source):
        slot = unit - input_pair(target, shares, modules, rank)
        return pltpu.make_async_remote_copy(
            src_ref=part_in.at[pl.ds(unit * rank, rank)],
            dst_ref=got_in.at[source, pl.ds(slot * rank, rank)],
            send_sem=in_send.at[unit, target],
            recv_sem=in_recv.at[source, slot],
            device_id=(me_dp, target),
            device_id_type=MESH,
        )

    pieces = []
    for target in range(shares):
        low, high = target * rows, (target + 1) * rows
        number = 0
        for module in range(modules):
            first, end = max(low, module * rank), min(high, (module + 1) * rank)
            if first < end:
                pieces.append((module, first, end - first, target, number))
                number += 1

    def out_copy(index, source):
        module, first, size, target, number = pieces[index]
        return pltpu.make_async_remote_copy(
            src_ref=part_out.at[pl.ds(first, size)],
            dst_ref=got_out.at[source, pl.ds(first - target * rows, size)],
            send_sem=out_send.at[index],
            recv_sem=out_recv.at[source, number],
            device_id=(me_dp, target),
            device_id_type=MESH,
        )

    def in_targets(unit):
        return [
            t for t in range(shares) if 0 <= unit - input_pair(t, shares, modules, rank) <= 1
        ]

    def send_unit(unit):
        if unit < 4:
            for target in in_targets(unit):
                @pl.when(me != target)
                def _():
                    in_copy(unit, target, me).start()
        else:
            for index, entry in enumerate(pieces):
                if entry[0] == unit - 4:
                    @pl.when(me != entry[3])
                    def _():
                        out_copy(index, me).start()

    def store(unit, columns, value):
        if unit < 4:
            part_in[pl.ds(unit * rank, rank), columns] = value.T
        else:
            part_out[pl.ds((unit - 4) * rank, rank), columns] = value.T

    def project(features, basis):
        return lax.dot_general(features, basis, NT, preferred_element_type=jnp.float32)

    for number, (kind, _, _, basis, basis_at, unit, chunk, slot) in enumerate(steps):
        need_basis(basis)
        load(number).wait()
        whole = pl.ds(0, tokens)
        if kind == "n":
            store(unit, whole, project(narrow[slot], basis[basis_at]))
        elif kind == "k":
            store(unit, whole, project(kv[0], basis[0]))
            store(unit + 1, whole, project(kv[1], basis[1]))
        else:
            weights = basis[...] if basis_at is None else basis[basis_at]
            store(unit, pl.ds(chunk * CHUNK, CHUNK), project(wide[slot], weights))
        if number + SLOTS < len(steps):
            load(number + SLOTS).start()
        if number == 0:
            pl.semaphore_wait(barrier, total - 1)
            for j in range(GROUP):
                @pl.when(lane != j)
                def _():
                    for t in range(shares):
                        test_copy(j, t, lane).start()
            for t in range(shares):
                own_test(t).start()
        if kind == "k":
            send_unit(unit)
            send_unit(unit + 1)
        elif kind == "n" or chunk == last_chunk:
            send_unit(unit)

    first_in = 0
    for t in range(1, shares):
        step_up = input_pair(t, shares, modules, rank) - input_pair(t - 1, shares, modules, rank)
        if step_up:
            first_in = first_in + step_up * (me >= t).astype(jnp.int32)
    sum_in = part_in[pl.ds(pl.multiple_of(first_in * rank, 8), 2 * rank), :]
    sum_out = part_out[pl.ds(pl.multiple_of(me * rows, 8), rows), :]
    for target in range(shares):
        @pl.when(me == target)
        def _():
            low = input_pair(target, shares, modules, rank)
            for hop in range(1, shares):
                source = (target + hop) % shares
                for unit in (low, low + 1):
                    in_copy(unit, target, source).wait_recv()
                for index, entry in enumerate(pieces):
                    if entry[3] == target:
                        out_copy(index, source).wait_recv()
    for hop in range(1, shares):
        source = (me + hop) % shares
        sum_in = sum_in + got_in[source]
        sum_out = sum_out + got_out[source]

    in_hi = sum_in.astype(jnp.bfloat16)
    in_lo = (sum_in - in_hi.astype(jnp.float32)).astype(jnp.bfloat16)
    out_hi = sum_out.astype(jnp.bfloat16)
    out_lo = (sum_out - out_hi.astype(jnp.float32)).astype(jnp.bfloat16)
    position = lax.broadcasted_iota(jnp.int32, (2 * rank, tokens), 1)
    begin = jnp.int32(0)
    for e in range(examples):
        finish = begin + lengths[0, e]
        member = jnp.logical_and(position >= begin, position < finish).astype(jnp.float32)
        member = member.astype(jnp.bfloat16)
        begin = finish
        hi, lo = in_hi * member, in_lo * member
        for s in range(2):
            r_hi[s, pl.ds(e * rank, rank), :] = hi[s * rank:(s + 1) * rank]
            r_lo[s, pl.ds(e * rank, rank), :] = lo[s * rank:(s + 1) * rank]

    flat_row = me * rows + lax.broadcasted_iota(jnp.int32, (rows, 2 * rank), 0)
    source_of = jnp.zeros((rows, 2 * rank), jnp.int32)
    for module in range(1, modules):
        jump = SOURCES[module] - SOURCES[module - 1]
        if jump:
            source_of = source_of + jump * (flat_row >= module * rank).astype(jnp.int32)
    is_first = source_of == first_in
    damped = eigen[pl.ds(pl.multiple_of(me * rows, 8), rows), :] + damping
    damped = jnp.concatenate([damped, damped], axis=1)
    left = lax.broadcasted_iota(jnp.int32, (pairs, 2 * rank), 1) < rank
    for block in range(examples // 2):
        both = []
        for s in range(2):
            hi = r_hi[s, pl.ds(block * 2 * rank, 2 * rank), :]
            lo = r_lo[s, pl.ds(block * 2 * rank, 2 * rank), :]
            both.append(
                lax.dot_general(out_hi, hi, NT, preferred_element_type=jnp.float32)
                + (
                    lax.dot_general(out_hi, lo, NT, preferred_element_type=jnp.float32)
                    + lax.dot_general(out_lo, hi, NT, preferred_element_type=jnp.float32)
                )
            )
        grads[block] = jnp.where(is_first, both[0], both[1]) / damped
        even = grads[block, pl.ds(0, pairs, stride=2), :]
        odd = grads[block, pl.ds(1, pairs, stride=2), :]
        scaled_f[:, 2 * block, :] = jnp.where(left, even, pltpu.roll(odd, rank, 1))
        scaled_f[:, 2 * block + 1, :] = jnp.where(left, pltpu.roll(even, rank, 1), odd)
    scaled[...] = scaled_f[...].astype(jnp.bfloat16)

    def grad_copy(k):
        other = (ident + k) % total
        other_dp = other // shares
        return pltpu.make_async_remote_copy(
            src_ref=scaled.at[pl.ds((other_dp % GROUP) * piece, piece)],
            dst_ref=gathered.at[me, me_dp],
            send_sem=grad_send.at[k],
            recv_sem=grad_recv.at[ident],
            device_id=(other_dp, other % shares),
            device_id_type=MESH,
        )

    def grad_arrival(k):
        other = (ident + k) % total
        other_dp = other // shares
        return pltpu.make_async_remote_copy(
            src_ref=scaled.at[pl.ds(0, piece)],
            dst_ref=gathered.at[other % shares, other_dp],
            send_sem=grad_send.at[k],
            recv_sem=grad_recv.at[other],
            device_id=(other_dp, other % shares),
            device_id_type=MESH,
        )

    def start_grad(k, carry):
        grad_copy(k).start()
        return carry

    lax.fori_loop(1, total, start_grad, 0)
    own_grad = pltpu.make_async_copy(
        scaled.at[pl.ds(lane * piece, piece)], gathered.at[me, me_dp], grad_local
    )
    own_grad.start()

    for unit in range(4):
        for target in in_targets(unit):
            @pl.when(me != target)
            def _():
                in_copy(unit, target, me).wait_send()
    for index, entry in enumerate(pieces):
        @pl.when(me != entry[3])
        def _():
            out_copy(index, me).wait_send()
    for j in range(GROUP):
        @pl.when(lane != j)
        def _():
            for t in range(shares):
                test_copy(j, t, lane).wait_send()
                test_copy(j, t, j).wait_recv()
    for t in range(shares):
        own_test(t).wait()
    own_grad.wait()

    def finish_grad(k, carry):
        grad_arrival(k).wait_recv()
        return carry

    lax.fori_loop(1, total, finish_grad, 0)

    for t in range(shares):
        for r in range(piece):
            tile = gathered[t, :, r].astype(jnp.float32).reshape(dp * examples, 2 * rank)
            spread[:, pl.ds((t * piece + r) * 2 * rank, 2 * rank)] = tile.astype(jnp.bfloat16)
    queries = tests[...].reshape(GROUP * tests.shape[1], tests.shape[2])
    part = lax.dot_general(queries, spread[...], NT, preferred_element_type=jnp.float32)
    partial[...] = part.reshape(partial.shape)

    def fin_copy(j, source_lane):
        return pltpu.make_async_remote_copy(
            src_ref=partial.at[j],
            dst_ref=got_partial.at[source_lane],
            send_sem=fin_send.at[j],
            recv_sem=fin_recv.at[source_lane],
            device_id=(group_at + j, me),
            device_id_type=MESH,
        )

    for j in range(GROUP):
        @pl.when(lane != j)
        def _():
            fin_copy(j, lane).start()

    def drain_grad(k, carry):
        grad_copy(k).wait_send()
        return carry

    lax.fori_loop(1, total, drain_grad, 0)
    result = partial[lane]
    for j in range(GROUP):
        @pl.when(lane != j)
        def _():
            fin_copy(j, j).wait_recv()
    for hop in range(1, GROUP):
        result = result + got_partial[(lane + hop) % GROUP]
    scores[...] = result
    for j in range(GROUP):
        @pl.when(lane != j)
        def _():
            fin_copy(j, lane).wait_send()


def shards(dp, shares, *arrays):
    (attention, mixing, feedforward, hidden, query, keyvalue, mixing_g, gateup, down,
     input_bases, hidden_basis, output_bases, keyvalue_bases, gateup_bases,
     eigenvalues, lengths, test) = arrays
    tokens, narrow_width = attention.shape
    wide_width = hidden.shape[1]
    rank = input_bases.shape[1]
    modules = len(SOURCES)
    rows = modules * rank // shares
    examples = lengths.shape[1]
    queries, flat = test.shape
    pairs = rows // 2
    piece = pairs // GROUP
    total = dp * shares
    f32, bf16 = jnp.float32, jnp.bfloat16
    V = pltpu.VMEM
    dma = pltpu.SemaphoreType.DMA
    eigen = eigenvalues.reshape(modules * rank, rank)
    any_spec = pl.BlockSpec(memory_space=pl.ANY)
    vmem_spec = pl.BlockSpec(memory_space=V)
    sizes = [a.size * a.dtype.itemsize for a in arrays]
    return pl.pallas_call(
        functools.partial(body, dp, shares),
        out_shape=jax.ShapeDtypeStruct((queries, dp * examples), f32),
        in_specs=[any_spec] * 14
        + [vmem_spec, pl.BlockSpec(memory_space=pltpu.SMEM), any_spec],
        out_specs=vmem_spec,
        scratch_shapes=[
            V((SLOTS, tokens, narrow_width), bf16),
            V((SLOTS, CHUNK, wide_width), bf16),
            V(keyvalue.shape, bf16),
            V(input_bases.shape, bf16),
            V(hidden_basis.shape, bf16),
            V(output_bases.shape, bf16),
            V(keyvalue_bases.shape, bf16),
            V(gateup_bases.shape, bf16),
            V((4 * rank, tokens), f32),
            V((modules * rank, tokens), f32),
            V((shares, 2 * rank, tokens), f32),
            V((shares, rows, tokens), f32),
            V((GROUP, queries, flat // GROUP), bf16),
            V((2, examples * rank, tokens), bf16),
            V((2, examples * rank, tokens), bf16),
            V((examples // 2, rows, 2 * rank), f32),
            V((pairs, examples, 2 * rank), f32),
            V((pairs, examples, 2 * rank), bf16),
            V((shares, dp, piece, examples, 2 * rank), bf16),
            V((dp * examples, flat // GROUP), bf16),
            V((GROUP, queries, dp * examples), f32),
            V((GROUP, queries, dp * examples), f32),
            dma((SLOTS,)),
            dma((5,)),
            dma((4, shares)),
            dma((shares, 2)),
            dma((4 * shares,)),
            dma((shares, 4)),
            dma((GROUP, shares)),
            dma((GROUP, shares)),
            dma((shares,)),
            dma((total,)),
            dma((total,)),
            dma,
            dma((GROUP,)),
            dma((GROUP,)),
        ],
        compiler_params=pltpu.CompilerParams(
            collective_id=0, has_side_effects=True, vmem_limit_bytes=56 * 1024 * 1024
        ),
        cost_estimate=pl.CostEstimate(
            flops=2 * rank * sum(sizes[:9]) // 2, bytes_accessed=sum(sizes), transcendentals=0
        ),
    )(attention, mixing, feedforward, hidden, query, keyvalue, mixing_g, gateup, down,
      input_bases, hidden_basis, output_bases, keyvalue_bases, gateup_bases,
      eigen, lengths, test)


def solution(mesh):
    in_specs = (
        P("dp", "tensor"),
        P("dp", "tensor"),
        P("dp", "tensor"),
        P("dp", "tensor"),
        P("dp", "tensor"),
        P(None, "dp", "tensor"),
        P("dp", "tensor"),
        P(None, "dp", "tensor"),
        P("dp", "tensor"),
        P(None, None, "tensor"),
        P(None, "tensor"),
        P(None, None, "tensor"),
        P(None, None, "tensor"),
        P(None, None, "tensor"),
        P(),
        P("dp", None),
        P(("dp", "tensor"), None),
    )
    out_specs = P(("dp", "tensor"), None)
    run = functools.partial(shards, mesh.shape["dp"], mesh.shape["tensor"])
    return jax.shard_map(run, mesh=mesh, in_specs=in_specs, out_specs=out_specs, check_vma=False)
```
